32 devices in a mesh: grp: 2 (over y), seq: 4 (over z), wt: 2 (over x), head: 2 (over core).
Axes of the slice: x: 2, y: 2, z: 4, core: 2. Of those that a mesh axis runs over, the one named last changes fastest.
Arguments:
- hidden: bfloat16 [2048, 2048], P(('grp', 'seq', 'wt'), 'head'), parts along dimension 0, may hold values from -6 to 6
- norm_gain: float32 [2048], replicated, may hold values from 0.1 to 1.9
- w_proj_x: bfloat16 [2048, 4096], P('wt', 'head'), may hold values from -0.125 to 0.125
- w_proj_bc: bfloat16 [2048, 512], P('wt', 'head'), may hold values from -0.125 to 0.125
- w_proj_dt: bfloat16 [2048, 32], P('wt', 'head'), may hold values from -0.125 to 0.125
- dt_bias: float32 [32], P('head'), may hold values from -4 to -1
- a_log: float32 [32], P('head'), may hold values from -20 to 1
- d_skip: float32 [32], P('head'), may hold values from 0.5 to 1.5
- inner_gain: float32 [4096], P('head'), may hold values from 0.1 to 1.9
- w_out: bfloat16 [4096, 2048], P('head', 'wt'), may hold values from -0.09375 to 0.09375
- lengths: int32 [16], P(('grp', 'seq', 'wt')), parts along dimension 0, may hold values from 1 to 128, 768 in all
- mix_index: int32 [16, 4], P(('grp', 'seq', 'wt')), parts along dimension 0, may hold values from 0 to 7, as said below
- mix_gain: float32 [16, 4], P(('grp', 'seq', 'wt')), parts along dimension 0, may hold values from -0.5 to 0.5
Outputs:
- layer_out: bfloat16 [2048, 2048], P(('grp', 'seq', 'wt'), 'head'), parts along dimension 0
The draws below stay inside these ranges and needn't reach their ends.
There are 2 independent parts, one for each index of `grp`. The reference program is written for one: setup_inputs(seed, part) draws one part's arguments, and reference() takes and returns one part's arrays. A program takes and returns all parts, laid end to end along the dimension named above; an argument that names none is the same for every part. Nothing has to cross between parts.
Inputs may be any that keep to these rules, and one draw needn't show every extreme that they name: `mix_index`: each listed block belongs to the same shard of 128 positions as its row's block or to one of the two shards next to it.
All inputs are finite; a program needn't handle non-finite values. No bound on the sum of `lengths` on one device may be relied on, other than what follows from the above.
Results may differ from the reference program's by a relative error of at most 0.0065.
Values may be sent and summed in bfloat16 or wider, within the bound.
A program may use at most 320 MiB of HBM per device.

```python
import math
import jax
import jax.numpy as jnp
import numpy as np
from jax import lax

D = 2048
H = 32
P_SIZE = 128
N = 128
NG = 2
SPAN = 128
BLK = 128
KB = 4
TOK_DEV = 128
HP = 4096
SHARDS = 8
TOKENS = 1024
NBLK = 8


def draw_a_log(key, part):
    first_key, second_key, third_key = jax.random.split(key, 3)
    slow_share = 0.5
    choose_slow = jax.random.uniform(first_key, (H,)) < slow_share
    slow_values = jnp.log(0.2 / TOKENS) + jax.random.uniform(second_key, (H,)) * jnp.log(5.0)
    fast_values = jnp.log(0.03) + jax.random.uniform(third_key, (H,)) * (jnp.log(2.0) - jnp.log(0.03))
    return jnp.where(choose_slow, slow_values, fast_values).astype(jnp.float32)


def draw_mix_index(key, part):
    first_key, second_key = jax.random.split(jax.random.fold_in(key, 7), 2)
    per_shard = TOK_DEV // BLK
    shard_count = TOKENS // TOK_DEV
    owners = jnp.arange(NBLK, dtype=jnp.int32) // per_shard
    offsets = jax.random.randint(first_key, (NBLK, KB), -1, 2)
    sources = jnp.clip(owners[:, None] + offsets, 0, shard_count - 1)
    within = jax.random.randint(second_key, (NBLK, KB), 0, per_shard)
    return (sources * per_shard + within).astype(jnp.int32)


def block_scale(own_key, dims, cuts, low, high):
    def one(dim, blocks):
        steps = jax.random.uniform(jax.random.fold_in(jax.random.fold_in(own_key, 6), dim), (blocks,), jnp.float32, low / len(cuts), high / len(cuts))
        return jnp.repeat(jnp.exp(steps), dims[dim] // blocks).reshape((-1,) + (1,) * (len(dims) - dim - 1))

    level = one(*cuts[0])
    for cut in cuts[1:]:
        level = level * one(*cut)
    return level


def length_profile(amount, total, reach, slope):
    weights = [(1 << 20) // math.isqrt(rank ** slope) + 1 for rank in range(2, amount + 1)]
    spare, given = total - reach - (amount - 1), [1] * (amount - 1)
    while spare > 0:
        movable = [i for i in range(amount - 1) if given[i] < reach]
        mass, budget = sum([weights[i] for i in movable]), spare
        for i in movable:
            addition = min(reach - given[i], max(1, budget * weights[i] // mass), spare)
            given[i] = given[i] + addition
            spare = spare - addition
    return np.array([reach] + given)


def uneven_parts(rng, count, total, limit, slope):
    if count == 2:
        one = jax.random.randint(rng, (), max(1, total - limit), min(limit, total - 1) + 1)
        return jnp.stack([one, total - one])
    sizes = jnp.asarray(length_profile(count, total, limit, slope), jnp.int32)
    pairs = (count - 1) // 2
    donor, receiver = sizes[1:1 + 2 * pairs:2], sizes[2:2 + 2 * pairs:2]
    margin = jnp.minimum(donor - 1, limit - receiver)
    moved = jax.random.randint(jax.random.fold_in(rng, 1), (pairs,), 0, 1 << 20) % (margin + 1)
    sizes = sizes.at[1:1 + 2 * pairs:2].set(donor - moved).at[2:2 + 2 * pairs:2].set(receiver + moved)
    return sizes[jax.random.permutation(jax.random.fold_in(rng, 2), count)]


def bell_draw(key, extent, scale, bound, cuts=(), kind=jnp.bfloat16):
    gain = block_scale(key, extent, cuts, -0.22, 0.18) if cuts else 1.0
    drawn = jax.random.normal(key, extent, jnp.float32) * scale * gain
    return jnp.minimum(jnp.maximum(drawn, -bound), bound).astype(kind)


def setup_inputs(seed: int = 0, part: int = 0) -> dict:
    key_of = jax.random.split(jax.random.key(seed), 14)
    own_keys = jax.random.split(jax.random.fold_in(key_of[13], part), 14)
    return {
        "hidden": bell_draw(own_keys[0], (TOKENS, D), 1.0, 6.0, ((0, 8), (1, 2))),
        "norm_gain": jnp.clip(1.0 + 0.18 * jax.random.normal(key_of[1], (D,), jnp.float32), 0.1, 1.9),
        "w_proj_x": bell_draw(key_of[2], (D, HP), D ** -0.5, 0.125, ((0, 2), (1, 2))),
        "w_proj_bc": bell_draw(key_of[3], (D, 2 * NG * N), D ** -0.5, 0.125, ((0, 2), (1, 2))),
        "w_proj_dt": bell_draw(key_of[4], (D, H), D ** -0.5, 0.125, ((0, 2), (1, 2))),
        "dt_bias": jnp.clip(-4.0 + 3.0 * jax.random.uniform(key_of[5], (H,), jnp.float32) ** block_scale(key_of[5], (H,), ((0, 2),), -0.2, 0.2), -4.0, -1.0),
        "a_log": draw_a_log(jax.random.fold_in(key_of[13], 71), part),
        "d_skip": jnp.clip(0.5 + 1.0 * jax.random.uniform(key_of[7], (H,), jnp.float32) ** block_scale(key_of[7], (H,), ((0, 2),), -0.2, 0.2), 0.5, 1.5),
        "inner_gain": jnp.clip(1.0 + 0.18 * jax.random.normal(key_of[8], (HP,), jnp.float32), 0.1, 1.9),
        "w_out": bell_draw(key_of[9], (HP, D), HP ** -0.5, 0.09375, ((0, 2), (1, 2))),
        "lengths": uneven_parts(own_keys[10], SHARDS, 3 * TOK_DEV * SHARDS // 4, TOK_DEV, 1).astype(jnp.int32),
        "mix_index": draw_mix_index(jax.random.fold_in(jax.random.fold_in(key_of[13], part), 71), part),
        "mix_gain": jnp.clip(jax.random.uniform(own_keys[12], (NBLK, KB), jnp.float32, -0.5, 0.5) * block_scale(own_keys[12], (NBLK, KB), ((0, 8),), -0.4, 0.0), -0.5, 0.5),
    }


eps_value = 1e-05
highest = lax.Precision.HIGHEST

def span_local(x_span, b_span, c_span, dt_span, log_span):
    cumulated = jnp.cumsum(log_span, axis=0)
    length = x_span.shape[0]
    rows_at = jnp.arange(length, dtype=jnp.int32)
    lower_part = rows_at[:, None] >= rows_at[None, :]
    difference = cumulated.T[:, :, None] - cumulated.T[:, None, :]
    decays = jnp.where(lower_part[None], jnp.exp(jnp.where(lower_part[None], difference, 0.0)), 0.0)
    scores = jnp.dot(c_span, b_span.T, precision=highest)
    weights = scores[None] * decays * dt_span.T[:, None, :]
    outputs = jnp.einsum('hts,shp->thp', weights, x_span, precision=highest)
    tail_decay = jnp.exp(cumulated[-1][None, :] - cumulated) * dt_span
    weighted_x = x_span * tail_decay[:, :, None]
    state_new = jnp.einsum('shp,sn->hpn', weighted_x, b_span, precision=highest)
    return (outputs, state_new, cumulated)

def from_state(c_span, cumulated, state_in):
    return jnp.einsum('tn,hpn->thp', c_span, state_in, precision=highest) * jnp.exp(cumulated)[:, :, None]

def reference(hidden, norm_gain, w_proj_x, w_proj_bc, w_proj_dt, dt_bias, a_log, d_skip, inner_gain, w_out, lengths, mix_index, mix_gain):
    floats = hidden.astype(jnp.float32)
    normed = (floats * lax.rsqrt(lax.optimization_barrier(jnp.mean(floats * floats, axis=-1, keepdims=True)) + eps_value) * norm_gain).astype(jnp.bfloat16)
    x_in = jax.nn.silu(jnp.dot(normed, w_proj_x, preferred_element_type=jnp.float32)).astype(jnp.bfloat16)
    bc_in = jax.nn.silu(jnp.dot(normed, w_proj_bc, preferred_element_type=jnp.float32)).astype(jnp.bfloat16)
    dt_raw = jnp.dot(normed, w_proj_dt, preferred_element_type=jnp.float32)
    places = jnp.arange(TOKENS, dtype=jnp.int32)
    live_mask = (places % TOK_DEV < lengths[places // TOK_DEV]).astype(jnp.float32)
    steps_dt = jax.nn.softplus(dt_raw + dt_bias) * live_mask[:, None]
    log_decay = -steps_dt * jnp.exp(a_log)
    per_group = H // NG
    spans = TOKENS // SPAN
    pieces = []
    for group_id in range(NG):
        first_head = group_id * per_group
        x_group = x_in[:, first_head * P_SIZE:(first_head + per_group) * P_SIZE].astype(jnp.float32).reshape(spans, SPAN, per_group, P_SIZE)
        b_group = bc_in[:, 2 * group_id * N:(2 * group_id + 1) * N].astype(jnp.float32).reshape(spans, SPAN, N)
        c_group = bc_in[:, (2 * group_id + 1) * N:(2 * group_id + 2) * N].astype(jnp.float32).reshape(spans, SPAN, N)
        dt_group = steps_dt[:, first_head:first_head + per_group].reshape(spans, SPAN, per_group)
        log_group = log_decay[:, first_head:first_head + per_group].reshape(spans, SPAN, per_group)

        def advance(carried, inputs):
            x_span, b_span, c_span, dt_span, log_span = inputs
            outputs, state_new, cumulated = span_local(x_span, b_span, c_span, dt_span, log_span)
            outputs = outputs + from_state(c_span, cumulated, carried)
            carried = jnp.exp(cumulated[-1])[:, None, None] * carried + state_new
            return (carried, outputs)
        initial = jnp.zeros((per_group, P_SIZE, N), jnp.float32)
        final_state, outputs = lax.scan(advance, initial, (x_group, b_group, c_group, dt_group, log_group))
        outputs = outputs.reshape(TOKENS, per_group, P_SIZE) + d_skip[first_head:first_head + per_group][None, :, None] * x_group.reshape(TOKENS, per_group, P_SIZE)
        scaling = lax.rsqrt(lax.optimization_barrier(jnp.mean(outputs * outputs, axis=-1, keepdims=True)) + eps_value)
        gain_rows = inner_gain[first_head * P_SIZE:(first_head + per_group) * P_SIZE].reshape(per_group, P_SIZE)
        pieces.append((outputs * scaling * gain_rows).astype(jnp.bfloat16).reshape(TOKENS, per_group * P_SIZE))
    y_norm = jnp.concatenate(pieces, axis=1)
    mixed_in = (floats + jnp.dot(y_norm, w_out, preferred_element_type=jnp.float32)).astype(jnp.bfloat16)
    blocks = mixed_in.reshape(NBLK, BLK, D)
    summed = blocks.astype(jnp.float32)
    for member in range(KB):
        summed = summed + mix_gain[:, member][:, None, None] * blocks[mix_index[:, member]].astype(jnp.float32)
    return summed.reshape(TOKENS, D).astype(jnp.bfloat16)
```

```python
import jax
import jax.numpy as jnp
from jax import lax
from jax.sharding import PartitionSpec as P

EPS = 1e-05
BF = jnp.bfloat16
F32 = jnp.float32


def rotated(pick, axis):
    n, me = lax.axis_size(axis), lax.axis_index(axis)
    got = [pick(me)]
    for k in range(1, n):
        got.append(lax.ppermute(pick((me + k) % n), axis, [(i, (i + k) % n) for i in range(n)]))
    return got


def returned(parts, axis):
    n = lax.axis_size(axis)
    return [parts[0]] + [
        lax.ppermute(parts[k], axis, [(i, (i - k) % n) for i in range(n)]) for k in range(1, n)
    ]


def dot(a, b):
    return jnp.dot(a, b, preferred_element_type=F32)


def body(hidden, norm_gain, w_x, w_bc, w_dt, dt_bias, a_log, d_skip, inner_gain, w_out,
         lengths, mix_index, mix_gain):
    tokens, half = hidden.shape
    width = norm_gain.shape[0]
    depth = w_x.shape[0]
    heads = w_dt.shape[1]
    size = w_x.shape[1] // heads
    state = w_bc.shape[1] // 2
    n_wt, me_wt, me_head = lax.axis_size("wt"), lax.axis_index("wt"), lax.axis_index("head")
    floats = hidden.astype(F32)
    whole = lax.all_gather(hidden, "head", axis=1, tiled=True)
    wf = whole.astype(F32)
    scale = lax.rsqrt(jnp.mean(wf * wf, axis=-1, keepdims=True) + EPS)
    normed = (wf * scale * norm_gain).astype(BF)
    rows = jnp.concatenate(
        rotated(lambda j: lax.dynamic_slice_in_dim(normed, j * depth, depth, axis=1), "wt"), axis=0
    )
    px, pb, pd = dot(rows, w_x).reshape(n_wt, tokens, -1), dot(rows, w_bc), dot(rows, w_dt)
    ps = jnp.concatenate([pb, pd], axis=1).reshape(n_wt, tokens, -1)
    x_parts = returned([px[0]] + [px[k].astype(BF) for k in range(1, n_wt)], "wt")
    s_parts = returned([ps[k] for k in range(n_wt)], "wt")
    x_sum = sum(p.astype(F32) for p in x_parts)
    s_sum = sum(s_parts)
    x_in = jax.nn.silu(x_sum).astype(BF)
    bc = jax.nn.silu(s_sum[:, : 2 * state]).astype(BF)
    b, c = bc[:, :state], bc[:, state:]
    live = (jnp.arange(tokens, dtype=jnp.int32) < lengths[0]).astype(F32)
    dt = jax.nn.softplus(s_sum[:, 2 * state:] + dt_bias) * live[:, None]
    log = -dt * jnp.exp(a_log)
    at = jnp.arange(tokens)
    lower = at[:, None] >= at[None, :]
    cum = jnp.dot(lower.astype(F32), log, precision=lax.Precision.HIGHEST)
    shards = lax.all_gather(cum[-1], ("seq", "wt"))
    xh = x_in.reshape(tokens, heads, size)
    diff = cum.T[:, :, None] - cum.T[:, None, :]
    decay = jnp.exp(jnp.where(lower[None], diff, -jnp.inf))
    scores = dot(c, b.T)
    weights = (scores[None] * decay * dt.T[:, None, :]).astype(BF)
    local = jnp.einsum("hts,shp->thp", weights, xh, preferred_element_type=F32)
    tail = jnp.exp(cum[-1][None, :] - cum) * dt
    fresh = jnp.einsum(
        "sn,shp->nhp", b, (xh.astype(F32) * tail[:, :, None]).astype(BF), preferred_element_type=F32
    )
    count = lax.axis_size(("seq", "wt"))
    me = lax.axis_index(("seq", "wt"))
    order = jnp.arange(count)
    total = fresh
    entering = lax.ppermute(fresh.astype(BF), ("seq", "wt"), [(i, i + 1) for i in range(count - 1)])
    entering = entering.astype(F32)
    span = 1
    while span < count - 1:
        decay_sum = jnp.sum(jnp.where(((order >= me - span) & (order < me))[:, None], shards, 0.0), axis=0)
        came = lax.ppermute(
            entering.astype(BF), ("seq", "wt"), [(i, i + span) for i in range(count - span)]
        )
        entering = entering + jnp.exp(decay_sum)[None, :, None] * came.astype(F32)
        span *= 2
    y = local + jnp.exp(cum)[:, :, None] * jnp.einsum(
        "tn,nhp->thp", c, entering.astype(BF), preferred_element_type=F32
    )
    y = y + d_skip[None, :, None] * xh.astype(F32)
    scaling = lax.rsqrt(jnp.mean(y * y, axis=-1, keepdims=True) + EPS)
    y_norm = (y * scaling * inner_gain.reshape(heads, size)).astype(BF).reshape(tokens, heads * size)
    y_rows = jnp.concatenate(rotated(lambda j: y_norm, "wt"), axis=0)
    po = dot(y_rows, w_out).astype(BF).reshape(n_wt, tokens, -1)
    o_parts = returned([po[k] for k in range(n_wt)], "wt")
    cols = w_out.shape[1]
    partial = jnp.zeros((tokens, width), BF)
    for k, part in enumerate(o_parts):
        partial = lax.dynamic_update_slice_in_dim(partial, part, ((me_wt + k) % n_wt) * cols, axis=1)
    keep = lax.dynamic_slice_in_dim(partial, me_head * half, half, axis=1)
    give = lax.dynamic_slice_in_dim(partial, (1 - me_head) * half, half, axis=1)
    other = lax.ppermute(give, "head", [(0, 1), (1, 0)])
    mixed = (floats + keep.astype(F32) + other.astype(F32)).astype(BF)
    prev = lax.ppermute(mixed, ("seq", "wt"), [(i, i + 1) for i in range(count - 1)])
    nxt = lax.ppermute(mixed, ("seq", "wt"), [(i + 1, i) for i in range(count - 1)])
    rel = mix_index[0] - me
    gain = [jnp.sum(jnp.where(rel == j, mix_gain[0], 0.0)) for j in (-1, 0, 1)]
    out = mixed.astype(F32) * (1.0 + gain[1]) + gain[0] * prev.astype(F32) + gain[2] * nxt.astype(F32)
    return out.astype(BF)


def solution(mesh):
    in_specs = (
        P(("grp", "seq", "wt"), "head"), P(), P("wt", "head"), P("wt", "head"), P("wt", "head"),
        P("head"), P("head"), P("head"), P("head"), P("head", "wt"),
        P(("grp", "seq", "wt")), P(("grp", "seq", "wt"), None), P(("grp", "seq", "wt"), None),
    )
    return jax.shard_map(
        body, mesh=mesh, in_specs=in_specs, out_specs=P(("grp", "seq", "wt"), "head"), check_vma=False
    )
```

```python
import jax
import jax.numpy as jnp
from jax import lax
from jax.sharding import PartitionSpec as P

EPS = 1e-05
BF = jnp.bfloat16
F32 = jnp.float32


def rotated(pick, axis):
    n, me = lax.axis_size(axis), lax.axis_index(axis)
    got = [pick(me)]
    for k in range(1, n):
        got.append(lax.ppermute(pick((me + k) % n), axis, [(i, (i + k) % n) for i in range(n)]))
    return got


def returned(parts, axis):
    n = lax.axis_size(axis)
    return [parts[0]] + [
        lax.ppermute(parts[k], axis, [(i, (i - k) % n) for i in range(n)]) for k in range(1, n)
    ]


def dot(a, b):
    return jnp.dot(a, b, preferred_element_type=F32)


def body(hidden, norm_gain, w_x, w_bc, w_dt, dt_bias, a_log, d_skip, inner_gain, w_out,
         lengths, mix_index, mix_gain):
    tokens, half = hidden.shape
    width = norm_gain.shape[0]
    depth = w_x.shape[0]
    heads = w_dt.shape[1]
    size = w_x.shape[1] // heads
    state = w_bc.shape[1] // 2
    n_wt, me_wt, me_head = lax.axis_size("wt"), lax.axis_index("wt"), lax.axis_index("head")
    floats = hidden.astype(F32)
    whole = lax.all_gather(hidden, "head", axis=1, tiled=True)
    wf = whole.astype(F32)
    scale = lax.rsqrt(jnp.mean(wf * wf, axis=-1, keepdims=True) + EPS)
    normed = (wf * scale * norm_gain).astype(BF)
    rows = jnp.concatenate(
        rotated(lambda j: lax.dynamic_slice_in_dim(normed, j * depth, depth, axis=1), "wt"), axis=0
    )
    px, pb, pd = dot(rows, w_x).reshape(n_wt, tokens, -1), dot(rows, w_bc), dot(rows, w_dt)
    ps = jnp.concatenate([pb, pd], axis=1).reshape(n_wt, tokens, -1)
    x_parts = returned([px[0]] + [px[k].astype(BF) for k in range(1, n_wt)], "wt")
    s_parts = returned([ps[k] for k in range(n_wt)], "wt")
    x_sum = sum(p.astype(F32) for p in x_parts)
    s_sum = sum(s_parts)
    x_in = jax.nn.silu(x_sum).astype(BF)
    bc = jax.nn.silu(s_sum[:, : 2 * state]).astype(BF)
    b, c = bc[:, :state], bc[:, state:]
    live = (jnp.arange(tokens, dtype=jnp.int32) < lengths[0]).astype(F32)
    dt = jax.nn.softplus(s_sum[:, 2 * state:] + dt_bias) * live[:, None]
    log = -dt * jnp.exp(a_log)
    at = jnp.arange(tokens)
    lower = at[:, None] >= at[None, :]
    cum = jnp.dot(lower.astype(F32), log, precision=lax.Precision.HIGHEST)
    xh = x_in.reshape(tokens, heads, size)
    diff = cum.T[:, :, None] - cum.T[:, None, :]
    decay = jnp.exp(jnp.where(lower[None], diff, -jnp.inf))
    scores = dot(c, b.T)
    weights = (scores[None] * decay * dt.T[:, None, :]).astype(BF)
    local = jnp.einsum("hts,shp->thp", weights, xh, preferred_element_type=F32)
    tail = jnp.exp(cum[-1][None, :] - cum) * dt
    fresh = jnp.einsum(
        "sn,shp->nhp", b, (xh.astype(F32) * tail[:, :, None]).astype(BF), preferred_element_type=F32
    )
    count = lax.axis_size(("seq", "wt"))
    me = lax.axis_index(("seq", "wt"))
    decay_sum = lax.ppermute(cum[-1], ("seq", "wt"), [(i, i + 1) for i in range(count - 1)])
    entering = lax.ppermute(fresh.astype(BF), ("seq", "wt"), [(i, i + 1) for i in range(count - 1)])
    entering = entering.astype(F32)
    span = 1
    while span < count - 1:
        decay_came = lax.ppermute(decay_sum, ("seq", "wt"), [(i, i + span) for i in range(count - span)])
        came = lax.ppermute(
            entering.astype(BF), ("seq", "wt"), [(i, i + span) for i in range(count - span)]
        )
        entering = entering + jnp.exp(decay_sum)[None, :, None] * came.astype(F32)
        decay_sum = decay_sum + decay_came
        span *= 2
    y = local + jnp.exp(cum)[:, :, None] * jnp.einsum(
        "tn,nhp->thp", c, entering.astype(BF), preferred_element_type=F32
    )
    y = y + d_skip[None, :, None] * xh.astype(F32)
    scaling = lax.rsqrt(jnp.mean(y * y, axis=-1, keepdims=True) + EPS)
    y_norm = (y * scaling * inner_gain.reshape(heads, size)).astype(BF).reshape(tokens, heads * size)
    y_rows = jnp.concatenate(rotated(lambda j: y_norm, "wt"), axis=0)
    po = dot(y_rows, w_out).astype(BF).reshape(n_wt, tokens, -1)
    o_parts = returned([po[k] for k in range(n_wt)], "wt")
    cols = w_out.shape[1]
    partial = jnp.zeros((tokens, width), BF)
    for k, part in enumerate(o_parts):
        partial = lax.dynamic_update_slice_in_dim(partial, part, ((me_wt + k) % n_wt) * cols, axis=1)
    keep = lax.dynamic_slice_in_dim(partial, me_head * half, half, axis=1)
    give = lax.dynamic_slice_in_dim(partial, (1 - me_head) * half, half, axis=1)
    other = lax.ppermute(give, "head", [(0, 1), (1, 0)])
    mixed = (floats + keep.astype(F32) + other.astype(F32)).astype(BF)
    prev = lax.ppermute(mixed, ("seq", "wt"), [(i, i + 1) for i in range(count - 1)])
    nxt = lax.ppermute(mixed, ("seq", "wt"), [(i + 1, i) for i in range(count - 1)])
    rel = mix_index[0] - me
    gain = [jnp.sum(jnp.where(rel == j, mix_gain[0], 0.0)) for j in (-1, 0, 1)]
    out = mixed.astype(F32) * (1.0 + gain[1]) + gain[0] * prev.astype(F32) + gain[2] * nxt.astype(F32)
    return out.astype(BF)


def solution(mesh):
    in_specs = (
        P(("grp", "seq", "wt"), "head"), P(), P("wt", "head"), P("wt", "head"), P("wt", "head"),
        P("head"), P("head"), P("head"), P("head"), P("head", "wt"),
        P(("grp", "seq", "wt")), P(("grp", "seq", "wt"), None), P(("grp", "seq", "wt"), None),
    )
    return jax.shard_map(
        body, mesh=mesh, in_specs=in_specs, out_specs=P(("grp", "seq", "wt"), "head"), check_vma=False
    )
```

```python
import functools

import jax
import jax.numpy as jnp
from jax import lax
from jax.experimental import pallas as pl
from jax.experimental.pallas import tpu as pltpu
from jax.sharding import PartitionSpec as P

EPS = 1e-05
BF = jnp.bfloat16
F32 = jnp.float32
MESH = pl.DeviceIdType.MESH
DMA = pltpu.SemaphoreType.DMA


def dot(a, b):
    return jnp.dot(a, b, preferred_element_type=F32)


def silu(v):
    return v * jax.nn.sigmoid(v)


def kernel(n_seq, n_wt, heads, hid, params, norm_gain, gains, wx_hbm, wbc, wdt, wo_hbm, out,
           hid_all, normed, rows, prod, small, wx, wo, x_in, cum_t, dt_t, fresh, e_in, e_out, yb,
           po, partial, hrec, mixed, prev_b, next_b,
           sem_w, sem_h, sem_r, sem_p, sem_s, sem_e, sem_y, sem_o, sem_g, sem_n):
    z, w, hd = lax.axis_index("seq"), lax.axis_index("wt"), lax.axis_index("head")
    tokens, half = hid.shape
    depth, cols = wx.shape[0], wo.shape[1]
    chan = wx.shape[1]
    count = n_seq * n_wt
    me = z * n_wt + w
    sib = {"head": 1 - hd}

    def peer(k):
        return {"wt": lax.rem(w + k + n_wt, n_wt)}

    def shard(step):
        at = lax.rem(me + step + count, count)
        return {"seq": at // n_wt, "wt": lax.rem(at, n_wt)}

    def remote(src, dst, sems, device):
        return pltpu.make_async_remote_copy(src_ref=src, dst_ref=dst, send_sem=sems.at[0],
                                            recv_sem=sems.at[1], device_id=device, device_id_type=MESH)

    load_x = pltpu.make_async_copy(wx_hbm, wx, sem_w.at[0])
    load_o = pltpu.make_async_copy(wo_hbm, wo, sem_w.at[1])
    load_x.start()
    load_o.start()
    barrier = pltpu.get_barrier_semaphore()
    for device in [sib, shard(1), shard(-1)] + [peer(k) for k in range(1, n_wt)]:
        pl.semaphore_signal(barrier, inc=1, device_id=device, device_id_type=MESH)
    pl.semaphore_wait(barrier, 3 + n_wt - 1)

    def block(at, size):
        return pl.ds(pl.multiple_of(at * size, 128), size)

    swap = remote(hid, hid_all.at[:, block(hd, half)], sem_h, sib)
    swap.start()
    hid_all[:, block(hd, half)] = hid[...]
    small[:n_wt] = jnp.zeros((n_wt,) + small.shape[1:], F32)

    @pl.when(me == 0)
    def _():
        e_in[...] = jnp.zeros_like(e_in)
        prev_b[...] = jnp.zeros_like(prev_b)

    @pl.when(me == count - 1)
    def _():
        next_b[...] = jnp.zeros_like(next_b)

    swap.wait()
    floats = hid_all[...].astype(F32)
    scale = lax.rsqrt(jnp.mean(floats * floats, axis=-1, keepdims=True) + EPS)
    normed[...] = (floats * scale * norm_gain[...]).astype(BF)
    sends = []
    for k in range(1, n_wt):
        sends.append(remote(normed.at[:, block(lax.rem(w + k, n_wt), depth)], rows.at[k],
                            sem_r.at[k], peer(k)))
        sends[-1].start()
    rows[0] = normed[:, block(w, depth)]
    load_x.wait()
    tile = min(512, chan)
    backs = []
    for k in range(n_wt):
        if k:
            sends[k - 1].wait()

        @pl.loop(0, chan // tile)
        def _(i):
            prod[k, :, block(i, tile)] = dot(rows[k], wx[:, block(i, tile)]).astype(BF)

        n_bc = wbc.shape[1]
        small[k, :, :n_bc] = dot(rows[k], wbc[...])
        small[k, :, n_bc:n_bc + heads] = dot(rows[k], wdt[...])
        if k:
            backs.append(remote(small.at[k], small.at[n_wt - 1 + k], sem_s.at[k], peer(-k)))
            backs.append(remote(prod.at[k], prod.at[n_wt - 1 + k], sem_p.at[k], peer(-k)))
            backs[-2].start()
            backs[-1].start()
    s_sum = small[0]
    for k in range(1, n_wt):
        backs[2 * k - 2].wait()
        s_sum = s_sum + small[n_wt - 1 + k]
    n_state = n_bc // 2
    bc = silu(s_sum[:, :n_bc])
    b, c = bc[:, :n_state].astype(BF), bc[:, n_state:].astype(BF)
    t_at = lax.broadcasted_iota(jnp.int32, (tokens, 128), 0)
    raw = s_sum[:, n_bc:] + params[0:1, :]
    soft = jnp.maximum(raw, 0.0) + jnp.log1p(jnp.exp(-jnp.abs(raw)))
    dt = jnp.where(t_at.astype(F32) < params[3:4, :], soft, 0.0)
    log = -dt * jnp.exp(params[1:2, :])
    lower = t_at >= lax.broadcasted_iota(jnp.int32, (tokens, tokens), 1)
    cum = jnp.dot(lower.astype(F32), log, precision=lax.Precision.HIGHEST, preferred_element_type=F32)
    cum_t[...] = cum.T
    dt_t[...] = dt.T
    b_f, c_f = b.astype(F32), c.astype(F32)
    b_t = b_f.T
    scores = dot(c, b_t.astype(BF))
    for k in range(1, n_wt):
        backs[2 * k - 1].wait()

    def head_cols(h):
        return block(h, 128)

    @pl.loop(0, heads)
    def _(h):
        at = head_cols(h)
        total = prod[0, :, at].astype(F32)
        for k in range(1, n_wt):
            total = total + prod[n_wt - 1 + k, :, at].astype(F32)
        x_h = silu(total).astype(BF)
        x_in[:, at] = x_h
        row = cum_t[pl.ds(h, 1), :]
        tail = jnp.exp(row[:, tokens - 1:] - row) * dt_t[pl.ds(h, 1), :]
        fresh[h] = dot((b_t * tail).astype(BF), x_h)

    def state_copy(h):
        return remote(e_out.at[h], e_in.at[h], sem_e.at[h], shard(1))

    def y_copy(h, k):
        at = head_cols(h)
        return remote(yb.at[0, :, at], yb.at[k, :, at], sem_y.at[h, k], peer(k))

    @pl.loop(0, heads)
    def _(h):
        at = head_cols(h)
        row = cum_t[pl.ds(h, 1), :]
        wide = jnp.broadcast_to(row, (tokens, tokens))
        tall = wide.T
        decay = jnp.exp(jnp.where(lower, tall - wide, -jnp.inf))
        x_h = x_in[:, at]
        y = dot((scores * decay * dt_t[pl.ds(h, 1), :]).astype(BF), x_h)
        y = y + gains[1:2, at] * x_h.astype(F32)
        grown = (c_f * jnp.exp(tall)).astype(BF)

        @pl.when(me > 0)
        def _():
            state_copy(h).wait_recv()

        entering = e_in[h]

        @pl.when(me < count - 1)
        def _():
            e_out[h] = (jnp.exp(row[:, tokens - 1:]) * entering.astype(F32) + fresh[h]).astype(BF)
            state_copy(h).start()

        y = y + dot(grown, entering)
        scaling = lax.rsqrt(jnp.mean(y * y, axis=-1, keepdims=True) + EPS)
        yb[0, :, at] = (y * scaling * gains[0:1, at]).astype(BF)
        for k in range(1, n_wt):
            y_copy(h, k).start()

    @pl.when(me < count - 1)
    def _():
        @pl.loop(0, heads)
        def _(h):
            state_copy(h).wait_send()

    load_o.wait()
    o_tile = min(256, cols)
    o_copies = []
    for k in range(n_wt):
        if k:
            @pl.loop(0, heads)
            def _(h):
                y_copy(h, k).wait()

        @pl.loop(0, cols // o_tile)
        def _(i):
            po[k, :, block(i, o_tile)] = dot(yb[k], wo[:, block(i, o_tile)]).astype(BF)

        if k:
            o_copies.append(remote(po.at[k], partial.at[:, block(w, cols)], sem_o.at[k], peer(-k)))
            o_copies[-1].start()
        else:
            partial[:, block(w, cols)] = po[0]
    for copy in o_copies:
        copy.wait()
    give = remote(partial.at[:, block(1 - hd, half)], hrec, sem_g, sib)
    give.start()
    base = hid[...].astype(F32) + partial[:, block(hd, half)].astype(F32)
    give.wait()
    mixed[...] = (base + hrec[...].astype(F32)).astype(BF)
    up = remote(mixed, prev_b, sem_n.at[0], shard(1))
    down = remote(mixed, next_b, sem_n.at[1], shard(-1))

    @pl.when(me < count - 1)
    def _():
        up.start()

    @pl.when(me > 0)
    def _():
        down.start()

    own = mixed[...].astype(F32) * params[5:6, 0:1]

    @pl.when(me > 0)
    def _():
        up.wait_recv()
        down.wait_send()

    @pl.when(me < count - 1)
    def _():
        down.wait_recv()
        up.wait_send()

    out[...] = (own + params[4:5, 0:1] * prev_b[...].astype(F32)
                + params[6:7, 0:1] * next_b[...].astype(F32)).astype(BF)


def body(hidden, norm_gain, w_x, w_bc, w_dt, dt_bias, a_log, d_skip, inner_gain, w_out,
         lengths, mix_index, mix_gain):
    tokens, half = hidden.shape
    width = norm_gain.shape[0]
    depth, chan = w_x.shape
    heads = w_dt.shape[1]
    size = chan // heads
    n_seq, n_wt = lax.axis_size("seq"), lax.axis_size("wt")
    cols = w_out.shape[1]
    rel = mix_index[0] - lax.axis_index(("seq", "wt"))
    mix = [jnp.sum(jnp.where(rel == j, mix_gain[0], 0.0)) for j in (-1, 0, 1)]
    pad = lambda v: jnp.pad(v, (0, 128 - heads))
    fill = lambda v: jnp.full((128,), v, F32)
    params = jnp.stack([pad(dt_bias), pad(a_log), fill(0.0), fill(lengths[0].astype(F32)),
                        fill(mix[0]), fill(1.0 + mix[1]), fill(mix[2]), fill(0.0)])
    gains = jnp.stack([inner_gain, jnp.repeat(d_skip, size)])
    slots = 2 * n_wt - 1
    vm, anyw = pl.BlockSpec(memory_space=pltpu.VMEM), pl.BlockSpec(memory_space=pl.ANY)
    V = pltpu.VMEM
    n_small = w_bc.shape[1] + 128
    return pl.pallas_call(
        functools.partial(kernel, n_seq, n_wt, heads),
        out_shape=jax.ShapeDtypeStruct((tokens, half), BF),
        in_specs=[vm, vm, vm, vm, anyw, vm, vm, anyw],
        out_specs=vm,
        scratch_shapes=[
            V((tokens, width), BF), V((tokens, width), BF), V((n_wt, tokens, depth), BF),
            V((slots, tokens, chan), BF), V((slots, tokens, n_small), F32),
            V((depth, chan), BF), V((chan, cols), BF), V((tokens, chan), BF),
            V((128, tokens), F32), V((128, tokens), F32), V((heads, size, size), F32),
            V((heads, size, size), BF), V((heads, size, size), BF), V((n_wt, tokens, chan), BF),
            V((n_wt, tokens, cols), BF), V((tokens, width), BF), V((tokens, half), BF),
            V((tokens, half), BF), V((tokens, half), BF), V((tokens, half), BF),
            DMA((2,)), DMA((2,)), DMA((n_wt, 2)), DMA((n_wt, 2)), DMA((n_wt, 2)), DMA((heads, 2)),
            DMA((heads, n_wt, 2)), DMA((n_wt, 2)), DMA((2,)), DMA((2, 2)),
        ],
        compiler_params=pltpu.CompilerParams(
            collective_id=0, has_side_effects=True, vmem_limit_bytes=48 * 2**20
        ),
    )(hidden, params, norm_gain[None, :], gains, w_x, w_bc, w_dt, w_out)


def solution(mesh):
    in_specs = (
        P(("grp", "seq", "wt"), "head"), P(), P("wt", "head"), P("wt", "head"), P("wt", "head"),
        P("head"), P("head"), P("head"), P("head"), P("head", "wt"),
        P(("grp", "seq", "wt")), P(("grp", "seq", "wt"), None), P(("grp", "seq", "wt"), None),
    )
    return jax.shard_map(
        body, mesh=mesh, in_specs=in_specs, out_specs=P(("grp", "seq", "wt"), "head"), check_vma=False
    )
```

```python
import functools

import jax
import jax.numpy as jnp
from jax import lax
from jax.experimental import pallas as pl
from jax.experimental.pallas import tpu as pltpu
from jax.sharding import PartitionSpec as P

EPS = 1e-05
BF = jnp.bfloat16
F32 = jnp.float32
MESH = pl.DeviceIdType.MESH
DMA = pltpu.SemaphoreType.DMA


def dot(a, b):
    return jnp.dot(a, b, preferred_element_type=F32)


def silu(v):
    return v * jax.nn.sigmoid(v)


def kernel(n_seq, n_wt, heads, hid_hbm, dt_bias, a_log, d_skip, lengths, mix_index, mix_gain, norm_gain,
           inner_gain, wx_hbm, wbc_hbm, wdt, wo_hbm, out, hid, wbc, params, y_loc, grow,
           hid_all, normed, rows, prod, small, wx, wo, cum_t, dt_t, fresh, e_in, e_out, yb,
           po, partial, hrec, mixed, prev_b, next_b,
           sem_w, sem_h, sem_r, sem_p, sem_s, sem_e, sem_y, sem_o, sem_g, sem_n):
    z, w, hd = lax.axis_index("seq"), lax.axis_index("wt"), lax.axis_index("head")
    tokens, half = hid.shape
    depth, cols = wx.shape[0], wo.shape[1]
    chan = wx.shape[1]
    count = n_seq * n_wt
    me = z * n_wt + w
    sib = {"head": 1 - hd}

    def peer(k):
        return {"wt": lax.rem(w + k + n_wt, n_wt)}

    def shard(step):
        at = lax.rem(me + step + count, count)
        return {"seq": at // n_wt, "wt": lax.rem(at, n_wt)}

    def remote(src, dst, sems, device):
        return pltpu.make_async_remote_copy(src_ref=src, dst_ref=dst, send_sem=sems.at[0],
                                            recv_sem=sems.at[1], device_id=device, device_id_type=MESH)

    load_x = pltpu.make_async_copy(wx_hbm, wx, sem_w.at[0])
    load_o = pltpu.make_async_copy(wo_hbm, wo, sem_w.at[1])
    load_h = pltpu.make_async_copy(hid_hbm, hid, sem_w.at[2])
    load_b = pltpu.make_async_copy(wbc_hbm, wbc, sem_w.at[3])
    load_h.start()
    load_b.start()
    load_x.start()
    load_o.start()
    params[...] = jnp.zeros_like(params)
    params[0:1, :heads] = dt_bias[...]
    params[1:2, :heads] = a_log[...]
    rel = [mix_index[0, k] - me for k in range(mix_index.shape[1])]
    mix = [sum(jnp.where(r == j, mix_gain[0, k], 0.0) for k, r in enumerate(rel)) for j in (-1, 0, 1)]
    barrier = pltpu.get_barrier_semaphore()
    for device in [sib, shard(1), shard(-1)] + [peer(k) for k in range(1, n_wt)]:
        pl.semaphore_signal(barrier, inc=1, device_id=device, device_id_type=MESH)
    pl.semaphore_wait(barrier, 3 + n_wt - 1)

    def block(at, size):
        return pl.ds(pl.multiple_of(at * size, 128), size)

    swap = remote(hid, hid_all.at[:, block(hd, half)], sem_h, sib)
    load_h.wait()
    swap.start()
    hid_all[:, block(hd, half)] = hid[...]
    small[:n_wt] = jnp.zeros((n_wt,) + small.shape[1:], F32)

    @pl.when(me == 0)
    def _():
        e_in[...] = jnp.zeros_like(e_in)
        prev_b[...] = jnp.zeros_like(prev_b)

    @pl.when(me == count - 1)
    def _():
        next_b[...] = jnp.zeros_like(next_b)

    swap.wait()
    floats = hid_all[...].astype(F32)
    scale = lax.rsqrt(jnp.mean(floats * floats, axis=-1, keepdims=True) + EPS)
    normed[...] = (floats * scale * norm_gain[...]).astype(BF)
    sends = []
    for k in range(1, n_wt):
        sends.append(remote(normed.at[:, block(lax.rem(w + k, n_wt), depth)], rows.at[k],
                            sem_r.at[k], peer(k)))
        sends[-1].start()
    rows[0] = normed[:, block(w, depth)]
    load_b.wait()
    load_x.wait()
    tile = min(512, chan)
    tiles = chan // tile
    backs = []

    def prod_copy(k, i):
        return remote(prod.at[k, :, block(i, tile)], prod.at[n_wt - 1 + k, :, block(i, tile)],
                      sem_p.at[k, i], peer(-k))

    for k in range(n_wt):
        if k:
            sends[k - 1].wait()

        n_bc = wbc.shape[1]
        small[k, :, :n_bc] = dot(rows[k], wbc[...])
        small[k, :, n_bc:n_bc + heads] = lax.dot_general(
            rows[k], wdt[...], (((1,), (1,)), ((), ())), preferred_element_type=F32)
        if k:
            backs.append(remote(small.at[k], small.at[n_wt - 1 + k], sem_s.at[k], peer(-k)))
            backs[-1].start()

        @pl.loop(0, tiles)
        def _(i):
            prod[k, :, block(i, tile)] = dot(rows[k], wx[:, block(i, tile)]).astype(BF)
            if k:
                prod_copy(k, i).start()

    s_sum = small[0]
    for k in range(1, n_wt):
        backs[k - 1].wait()
        s_sum = s_sum + small[n_wt - 1 + k]
    n_state = n_bc // 2
    bc = silu(s_sum[:, :n_bc])
    b, c = bc[:, :n_state].astype(BF), bc[:, n_state:].astype(BF)
    t_at = lax.broadcasted_iota(jnp.int32, (tokens, 128), 0)
    raw = s_sum[:, n_bc:] + params[0:1, :]
    soft = jnp.maximum(raw, 0.0) + jnp.log1p(jnp.exp(-jnp.abs(raw)))
    dt = jnp.where(t_at < lengths[0], soft, 0.0)
    log = -dt * jnp.exp(params[1:2, :])
    lower = t_at >= lax.broadcasted_iota(jnp.int32, (tokens, tokens), 1)
    cum = jnp.dot(lower.astype(F32), log, precision=lax.Precision.HIGHEST, preferred_element_type=F32)
    cum_t[...] = cum.T
    dt_t[...] = dt.T
    b_f, c_f = b.astype(F32), c.astype(F32)
    b_t = b_f.T
    scores = dot(c, b_t.astype(BF))

    def head_cols(h):
        return block(h, 128)

    def one_head(h):
        at = head_cols(h)
        total = prod[0, :, at].astype(F32)
        for k in range(1, n_wt):
            total = total + prod[n_wt - 1 + k, :, at].astype(F32)
        x_h = silu(total).astype(BF)
        row = cum_t[pl.ds(h, 1), :]
        dt_row = dt_t[pl.ds(h, 1), :]
        tail = jnp.exp(row[:, tokens - 1:] - row) * dt_row
        fresh[h] = dot((b_t * tail).astype(BF), x_h)
        wide = jnp.broadcast_to(row, (tokens, tokens))
        tall = wide.T
        decay = jnp.exp(jnp.where(lower, tall - wide, -jnp.inf))
        y = dot((scores * decay * dt_row).astype(BF), x_h)
        y_loc[:, at] = y + d_skip[h] * x_h.astype(F32)
        grow[h] = (c_f * jnp.exp(tall)).astype(BF)

    per_tile = tile // 128

    @pl.loop(0, tiles)
    def _(i):
        for k in range(1, n_wt):
            prod_copy(k, i).wait()
        for j in range(per_tile):
            one_head(i * per_tile + j)

    def state_copy(h):
        return remote(e_out.at[h], e_in.at[h], sem_e.at[h], shard(1))

    def y_copy(h, k):
        at = head_cols(h)
        return remote(yb.at[0, :, at], yb.at[k, :, at], sem_y.at[h, k], peer(k))

    @pl.loop(0, heads)
    def _(h):
        at = head_cols(h)
        row = cum_t[pl.ds(h, 1), :]
        @pl.when(me > 0)
        def _():
            state_copy(h).wait_recv()

        entering = e_in[h]

        @pl.when(me < count - 1)
        def _():
            e_out[h] = (jnp.exp(row[:, tokens - 1:]) * entering.astype(F32) + fresh[h]).astype(BF)
            state_copy(h).start()

        y = y_loc[:, at] + dot(grow[h], entering)
        scaling = lax.rsqrt(jnp.mean(y * y, axis=-1, keepdims=True) + EPS)
        yb[0, :, at] = (y * scaling * inner_gain[0:1, at]).astype(BF)
        for k in range(1, n_wt):
            y_copy(h, k).start()

    @pl.when(me < count - 1)
    def _():
        @pl.loop(0, heads)
        def _(h):
            state_copy(h).wait_send()

    load_o.wait()
    o_tile = min(256, cols)
    o_copies = []
    for k in range(n_wt):
        if k:
            @pl.loop(0, heads)
            def _(h):
                y_copy(h, k).wait()

        @pl.loop(0, cols // o_tile)
        def _(i):
            po[k, :, block(i, o_tile)] = dot(yb[k], wo[:, block(i, o_tile)]).astype(BF)

        if k:
            o_copies.append(remote(po.at[k], partial.at[:, block(w, cols)], sem_o.at[k], peer(-k)))
            o_copies[-1].start()
        else:
            partial[:, block(w, cols)] = po[0]
    for copy in o_copies:
        copy.wait()
    give = remote(partial.at[:, block(1 - hd, half)], hrec, sem_g, sib)
    give.start()
    base = hid[...].astype(F32) + partial[:, block(hd, half)].astype(F32)
    give.wait()
    mixed[...] = (base + hrec[...].astype(F32)).astype(BF)
    up = remote(mixed, prev_b, sem_n.at[0], shard(1))
    down = remote(mixed, next_b, sem_n.at[1], shard(-1))

    @pl.when(me < count - 1)
    def _():
        up.start()

    @pl.when(me > 0)
    def _():
        down.start()

    own = mixed[...].astype(F32) * (1.0 + mix[1])

    @pl.when(me > 0)
    def _():
        up.wait_recv()
        down.wait_send()

    @pl.when(me < count - 1)
    def _():
        down.wait_recv()
        up.wait_send()

    out[...] = (own + mix[0] * prev_b[...].astype(F32)
                + mix[2] * next_b[...].astype(F32)).astype(BF)


def body(hidden, norm_gain, w_x, w_bc, w_dt, dt_bias, a_log, d_skip, inner_gain, w_out,
         lengths, mix_index, mix_gain):
    tokens, half = hidden.shape
    width = norm_gain.shape[0]
    depth, chan = w_x.shape
    heads = w_dt.shape[1]
    size = chan // heads
    n_seq, n_wt = lax.axis_size("seq"), lax.axis_size("wt")
    cols = w_out.shape[1]
    slots = 2 * n_wt - 1
    vm, anyw = pl.BlockSpec(memory_space=pltpu.VMEM), pl.BlockSpec(memory_space=pl.ANY)
    V, sm = pltpu.VMEM, pl.BlockSpec(memory_space=pltpu.SMEM)
    n_small = w_bc.shape[1] + 128
    return pl.pallas_call(
        functools.partial(kernel, n_seq, n_wt, heads),
        out_shape=jax.ShapeDtypeStruct((tokens, half), BF),
        in_specs=[anyw, vm, vm, sm, sm, sm, sm, vm, vm, anyw, anyw, vm, anyw],
        out_specs=vm,
        scratch_shapes=[
            V((tokens, half), BF), V(w_bc.shape, BF), V((8, 128), F32), V((tokens, chan), F32),
            V((heads, tokens, size), BF),
            V((tokens, width), BF), V((tokens, width), BF), V((n_wt, tokens, depth), BF),
            V((slots, tokens, chan), BF), V((slots, tokens, n_small), F32),
            V((depth, chan), BF), V((chan, cols), BF),
            V((128, tokens), F32), V((128, tokens), F32), V((heads, size, size), F32),
            V((heads, size, size), BF), V((heads, size, size), BF), V((n_wt, tokens, chan), BF),
            V((n_wt, tokens, cols), BF), V((tokens, width), BF), V((tokens, half), BF),
            V((tokens, half), BF), V((tokens, half), BF), V((tokens, half), BF),
            DMA((4,)), DMA((2,)), DMA((n_wt, 2)), DMA((n_wt, chan // 128, 2)), DMA((n_wt, 2)), DMA((heads, 2)),
            DMA((heads, n_wt, 2)), DMA((n_wt, 2)), DMA((2,)), DMA((2, 2)),
        ],
        compiler_params=pltpu.CompilerParams(
            collective_id=0, has_side_effects=True, vmem_limit_bytes=63 * 2**20
        ),
    )(hidden, dt_bias[None, :], a_log[None, :], d_skip, lengths, mix_index, mix_gain, norm_gain[None, :],
      inner_gain[None, :], w_x, w_bc, w_dt.T, w_out)


def solution(mesh):
    in_specs = (
        P(("grp", "seq", "wt"), "head"), P(), P("wt", "head"), P("wt", "head"), P("wt", "head"),
        P("head"), P("head"), P("head"), P("head"), P("head", "wt"),
        P(("grp", "seq", "wt")), P(("grp", "seq", "wt"), None), P(("grp", "seq", "wt"), None),
    )
    return jax.shard_map(
        body, mesh=mesh, in_specs=in_specs, out_specs=P(("grp", "seq", "wt"), "head"), check_vma=False
    )
```

```python
import functools

import jax
import jax.numpy as jnp
from jax import lax
from jax.experimental import pallas as pl
from jax.experimental.pallas import tpu as pltpu
from jax.sharding import PartitionSpec as P

EPS = 1e-05
BF = jnp.bfloat16
F32 = jnp.float32
MESH = pl.DeviceIdType.MESH
DMA = pltpu.SemaphoreType.DMA


def dot(a, b):
    return jnp.dot(a, b, preferred_element_type=F32)


def silu(v):
    return v * jax.nn.sigmoid(v)


def kernel(n_seq, n_wt, heads, hid_hbm, dt_bias, a_log, d_skip, lengths, mix_index, mix_gain, norm_gain,
           inner_gain, wx_hbm, wbc_hbm, wdt, wo_hbm, out, hid, wbc, params, y_loc, grow,
           hid_all, normed, rows, prod, small, bcs, wx, wo, cum_t, dt_t, fresh, e_in, e_out, yb, yh,
           po, partial, hrec, mixed, prev_b, next_b,
           sem_w, sem_h, sem_r, sem_p, sem_s, sem_b, sem_e, sem_y, sem_o, sem_g, sem_n):
    z, w, hd = lax.axis_index("seq"), lax.axis_index("wt"), lax.axis_index("head")
    tokens, half = hid.shape
    depth, cols = wx.shape[0], wo.shape[1]
    chan = wx.shape[1]
    count = n_seq * n_wt
    me = z * n_wt + w
    sib = {"head": 1 - hd}

    def peer(k):
        return {"wt": lax.rem(w + k + n_wt, n_wt)}

    def shard(step):
        at = lax.rem(me + step + count, count)
        return {"seq": at // n_wt, "wt": lax.rem(at, n_wt)}

    def remote(src, dst, sems, device):
        return pltpu.make_async_remote_copy(src_ref=src, dst_ref=dst, send_sem=sems.at[0],
                                            recv_sem=sems.at[1], device_id=device, device_id_type=MESH)

    load_x = pltpu.make_async_copy(wx_hbm, wx, sem_w.at[0])
    load_o = pltpu.make_async_copy(wo_hbm, wo, sem_w.at[1])
    load_h = pltpu.make_async_copy(hid_hbm, hid, sem_w.at[2])
    load_b = pltpu.make_async_copy(wbc_hbm, wbc, sem_w.at[3])
    load_h.start()
    load_b.start()
    load_x.start()
    load_o.start()
    params[...] = jnp.zeros_like(params)
    params[0:1, :heads] = dt_bias[...]
    params[1:2, :heads] = a_log[...]
    rel = [mix_index[0, k] - me for k in range(mix_index.shape[1])]
    mix = [sum(jnp.where(r == j, mix_gain[0, k], 0.0) for k, r in enumerate(rel)) for j in (-1, 0, 1)]
    barrier = pltpu.get_barrier_semaphore()
    for device in [sib, shard(1), shard(-1)] + [peer(k) for k in range(1, n_wt)]:
        pl.semaphore_signal(barrier, inc=1, device_id=device, device_id_type=MESH)
    pl.semaphore_wait(barrier, 3 + n_wt - 1)

    def block(at, size):
        return pl.ds(pl.multiple_of(at * size, 128), size)

    swap = remote(hid, hid_all.at[:, block(hd, half)], sem_h, sib)
    load_h.wait()
    swap.start()
    hid_all[:, block(hd, half)] = hid[...]
    small[:n_wt] = jnp.zeros((n_wt,) + small.shape[1:], F32)

    @pl.when(me == 0)
    def _():
        e_in[...] = jnp.zeros_like(e_in)
        prev_b[...] = jnp.zeros_like(prev_b)

    @pl.when(me == count - 1)
    def _():
        next_b[...] = jnp.zeros_like(next_b)

    swap.wait()
    floats = hid_all[...].astype(F32)
    scale = lax.rsqrt(jnp.mean(floats * floats, axis=-1, keepdims=True) + EPS)
    normed[...] = (floats * scale * norm_gain[...]).astype(BF)
    sends = []
    for k in range(1, n_wt):
        sends.append(remote(normed.at[:, block(lax.rem(w + k, n_wt), depth)], rows.at[k],
                            sem_r.at[k], peer(k)))
        sends[-1].start()
    rows[0] = normed[:, block(w, depth)]
    load_b.wait()
    load_x.wait()
    tiles, tile = prod.shape[1], prod.shape[3]
    backs = []

    def prod_copy(k, i):
        return remote(prod.at[k, i], prod.at[n_wt - 1 + k, i],
                      sem_p.at[k, i], peer(-k))

    for k in range(n_wt):
        if k:
            sends[k - 1].wait()

        n_bc = wbc.shape[1]
        bcs[k] = dot(rows[k], wbc[...]).astype(BF)
        small[k, :, :heads] = lax.dot_general(
            rows[k], wdt[...], (((1,), (1,)), ((), ())), preferred_element_type=F32)
        if k:
            backs.append(remote(small.at[k], small.at[n_wt - 1 + k], sem_s.at[k], peer(-k)))
            backs.append(remote(bcs.at[k], bcs.at[n_wt - 1 + k], sem_b.at[k], peer(-k)))
            backs[-2].start()
            backs[-1].start()

        @pl.loop(0, tiles)
        def _(i):
            prod[k, i] = dot(rows[k], wx[:, block(i, tile)]).astype(BF)
            if k:
                prod_copy(k, i).start()

    s_sum, bc_sum = small[0], bcs[0].astype(F32)
    for k in range(1, n_wt):
        backs[2 * k - 2].wait()
        backs[2 * k - 1].wait()
        s_sum = s_sum + small[n_wt - 1 + k]
        bc_sum = bc_sum + bcs[n_wt - 1 + k].astype(F32)
    n_state = n_bc // 2
    bc = silu(bc_sum)
    b, c = bc[:, :n_state].astype(BF), bc[:, n_state:].astype(BF)
    t_at = lax.broadcasted_iota(jnp.int32, (tokens, 128), 0)
    raw = s_sum + params[0:1, :]
    soft = jnp.maximum(raw, 0.0) + jnp.log1p(jnp.exp(-jnp.abs(raw)))
    dt = jnp.where(t_at < lengths[0], soft, 0.0)
    log = -dt * jnp.exp(params[1:2, :])
    lower = t_at >= lax.broadcasted_iota(jnp.int32, (tokens, tokens), 1)
    cum = jnp.dot(lower.astype(F32), log, precision=lax.Precision.HIGHEST, preferred_element_type=F32)
    cum_t[...] = cum.T
    dt_t[...] = dt.T
    b_f, c_f = b.astype(F32), c.astype(F32)
    b_t = b_f.T
    scores = dot(c, b_t.astype(BF))

    def head_cols(h):
        return block(h, 128)

    def one_head(h, i, j):
        at, cut = head_cols(h), slice(j * 128, (j + 1) * 128)
        total = prod[0, i, :, cut].astype(F32)
        for k in range(1, n_wt):
            total = total + prod[n_wt - 1 + k, i, :, cut].astype(F32)
        x_h = silu(total).astype(BF)
        row = cum_t[pl.ds(h, 1), :]
        dt_row = dt_t[pl.ds(h, 1), :]
        tail = jnp.exp(row[:, tokens - 1:] - row) * dt_row
        fresh[h] = dot((b_t * tail).astype(BF), x_h)
        wide = jnp.broadcast_to(row, (tokens, tokens))
        tall = wide.T
        decay = jnp.exp(jnp.where(lower, tall - wide, -jnp.inf))
        y = dot((scores * decay * dt_row).astype(BF), x_h)
        y_loc[:, at] = y + d_skip[h] * x_h.astype(F32)
        grow[h] = (c_f * jnp.exp(tall)).astype(BF)

    per_tile = tile // 128

    @pl.loop(0, tiles)
    def _(i):
        for k in range(1, n_wt):
            prod_copy(k, i).wait()
        for j in range(per_tile):
            one_head(i * per_tile + j, i, j)

    def state_copy(h):
        return remote(e_out.at[h], e_in.at[h], sem_e.at[h], shard(1))

    def y_copy(h, k):
        return remote(yh.at[0, h], yh.at[k, h], sem_y.at[h, k], peer(k))

    @pl.loop(0, heads)
    def _(h):
        at = head_cols(h)
        row = cum_t[pl.ds(h, 1), :]
        @pl.when(me > 0)
        def _():
            state_copy(h).wait_recv()

        entering = e_in[h]

        @pl.when(me < count - 1)
        def _():
            e_out[h] = (jnp.exp(row[:, tokens - 1:]) * entering.astype(F32) + fresh[h]).astype(BF)
            state_copy(h).start()

        y = y_loc[:, at] + dot(grow[h], entering)
        scaling = lax.rsqrt(jnp.mean(y * y, axis=-1, keepdims=True) + EPS)
        y_h = (y * scaling * inner_gain[0:1, at]).astype(BF)
        yb[0, :, at] = y_h
        yh[0, h] = y_h
        for k in range(1, n_wt):
            y_copy(h, k).start()

    @pl.when(me < count - 1)
    def _():
        @pl.loop(0, heads)
        def _(h):
            state_copy(h).wait_send()

    load_o.wait()
    o_tile = min(256, cols)
    o_copies = []
    for k in range(n_wt):
        if k:
            @pl.loop(0, heads)
            def _(h):
                y_copy(h, k).wait()
                yb[k, :, head_cols(h)] = yh[k, h]

        @pl.loop(0, cols // o_tile)
        def _(i):
            po[k, :, block(i, o_tile)] = dot(yb[k], wo[:, block(i, o_tile)]).astype(BF)

        if k:
            o_copies.append(remote(po.at[k], partial.at[:, block(w, cols)], sem_o.at[k], peer(-k)))
            o_copies[-1].start()
        else:
            partial[:, block(w, cols)] = po[0]
    for copy in o_copies:
        copy.wait()
    give = remote(partial.at[:, block(1 - hd, half)], hrec, sem_g, sib)
    give.start()
    base = hid[...].astype(F32) + partial[:, block(hd, half)].astype(F32)
    give.wait()
    mixed[...] = (base + hrec[...].astype(F32)).astype(BF)
    up = remote(mixed, prev_b, sem_n.at[0], shard(1))
    down = remote(mixed, next_b, sem_n.at[1], shard(-1))

    @pl.when(me < count - 1)
    def _():
        up.start()

    @pl.when(me > 0)
    def _():
        down.start()

    own = mixed[...].astype(F32) * (1.0 + mix[1])

    @pl.when(me > 0)
    def _():
        up.wait_recv()
        down.wait_send()

    @pl.when(me < count - 1)
    def _():
        down.wait_recv()
        up.wait_send()

    out[...] = (own + mix[0] * prev_b[...].astype(F32)
                + mix[2] * next_b[...].astype(F32)).astype(BF)


def body(hidden, norm_gain, w_x, w_bc, w_dt, dt_bias, a_log, d_skip, inner_gain, w_out,
         lengths, mix_index, mix_gain):
    tokens, half = hidden.shape
    width = norm_gain.shape[0]
    depth, chan = w_x.shape
    heads = w_dt.shape[1]
    size = chan // heads
    n_seq, n_wt = lax.axis_size("seq"), lax.axis_size("wt")
    cols = w_out.shape[1]
    slots = 2 * n_wt - 1
    vm, anyw = pl.BlockSpec(memory_space=pltpu.VMEM), pl.BlockSpec(memory_space=pl.ANY)
    V, sm = pltpu.VMEM, pl.BlockSpec(memory_space=pltpu.SMEM)
    tile = min(512, chan)
    return pl.pallas_call(
        functools.partial(kernel, n_seq, n_wt, heads),
        out_shape=jax.ShapeDtypeStruct((tokens, half), BF),
        in_specs=[anyw, vm, vm, sm, sm, sm, sm, vm, vm, anyw, anyw, vm, anyw],
        out_specs=vm,
        scratch_shapes=[
            V((tokens, half), BF), V(w_bc.shape, BF), V((8, 128), F32), V((tokens, chan), F32),
            V((heads, tokens, size), BF),
            V((tokens, width), BF), V((tokens, width), BF), V((n_wt, tokens, depth), BF),
            V((slots, chan // tile, tokens, tile), BF), V((slots, tokens, 128), F32),
            V((slots, tokens, w_bc.shape[1]), BF),
            V((depth, chan), BF), V((chan, cols), BF),
            V((128, tokens), F32), V((128, tokens), F32), V((heads, size, size), F32),
            V((heads, size, size), BF), V((heads, size, size), BF), V((n_wt, tokens, chan), BF),
            V((n_wt, heads, tokens, size), BF),
            V((n_wt, tokens, cols), BF), V((tokens, width), BF), V((tokens, half), BF),
            V((tokens, half), BF), V((tokens, half), BF), V((tokens, half), BF),
            DMA((4,)), DMA((2,)), DMA((n_wt, 2)), DMA((n_wt, chan // 128, 2)), DMA((n_wt, 2)), DMA((n_wt, 2)), DMA((heads, 2)),
            DMA((heads, n_wt, 2)), DMA((n_wt, 2)), DMA((2,)), DMA((2, 2)),
        ],
        compiler_params=pltpu.CompilerParams(
            collective_id=0, has_side_effects=True, vmem_limit_bytes=63 * 2**20
        ),
    )(hidden, dt_bias[None, :], a_log[None, :], d_skip, lengths, mix_index, mix_gain, norm_gain[None, :],
      inner_gain[None, :], w_x, w_bc, w_dt.T, w_out)


def solution(mesh):
    in_specs = (
        P(("grp", "seq", "wt"), "head"), P(), P("wt", "head"), P("wt", "head"), P("wt", "head"),
        P("head"), P("head"), P("head"), P("head"), P("head", "wt"),
        P(("grp", "seq", "wt")), P(("grp", "seq", "wt"), None), P(("grp", "seq", "wt"), None),
    )
    return jax.shard_map(
        body, mesh=mesh, in_specs=in_specs, out_specs=P(("grp", "seq", "wt"), "head"), check_vma=False
    )
```

```python
import functools

import jax
import jax.numpy as jnp
from jax import lax
from jax.experimental import pallas as pl
from jax.experimental.pallas import tpu as pltpu
from jax.sharding import PartitionSpec as P

EPS = 1e-05
BF = jnp.bfloat16
F32 = jnp.float32
MESH = pl.DeviceIdType.MESH
DMA = pltpu.SemaphoreType.DMA


def dot(a, b):
    return jnp.dot(a, b, preferred_element_type=F32)


def silu(v):
    return v * jax.nn.sigmoid(v)


def kernel(n_seq, n_wt, heads, hid_hbm, dt_bias, a_log, d_skip, lengths, mix_index, mix_gain, norm_gain,
           inner_gain, wx_hbm, wbc_hbm, wdt, wo_hbm, out, hid, wbc, params, y_loc, grow,
           hid_all, normed, rows, prod, small, bcs, wx, wo, cum_t, dt_t, fresh, e_in, e_out, yb, yh,
           po, partial, hrec, mixed, prev_b, next_b,
           sem_w, sem_h, sem_r, sem_p, sem_s, sem_b, sem_e, sem_y, sem_o, sem_g, sem_n):
    z, w, hd = lax.axis_index("seq"), lax.axis_index("wt"), lax.axis_index("head")
    tokens, half = hid.shape
    depth, cols = wx.shape[0], wo.shape[1]
    chan = wx.shape[1]
    count = n_seq * n_wt
    me = z * n_wt + w
    sib = {"head": 1 - hd}

    def peer(k):
        return {"wt": lax.rem(w + k + n_wt, n_wt)}

    def shard(step):
        at = lax.rem(me + step + count, count)
        return {"seq": at // n_wt, "wt": lax.rem(at, n_wt)}

    def remote(src, dst, sems, device):
        return pltpu.make_async_remote_copy(src_ref=src, dst_ref=dst, send_sem=sems.at[0],
                                            recv_sem=sems.at[1], device_id=device, device_id_type=MESH)

    load_x = pltpu.make_async_copy(wx_hbm, wx, sem_w.at[0])
    load_o = pltpu.make_async_copy(wo_hbm, wo, sem_w.at[1])
    load_h = pltpu.make_async_copy(hid_hbm, hid, sem_w.at[2])
    load_b = pltpu.make_async_copy(wbc_hbm, wbc, sem_w.at[3])
    load_h.start()
    load_b.start()
    load_x.start()
    load_o.start()
    params[...] = jnp.zeros_like(params)
    params[0:1, :heads] = dt_bias[...]
    params[1:2, :heads] = a_log[...]
    rel = [mix_index[0, k] - me for k in range(mix_index.shape[1])]
    mix = [sum(jnp.where(r == j, mix_gain[0, k], 0.0) for k, r in enumerate(rel)) for j in (-1, 0, 1)]
    barrier = pltpu.get_barrier_semaphore()
    for device in [sib, shard(1), shard(-1)] + [peer(k) for k in range(1, n_wt)]:
        pl.semaphore_signal(barrier, inc=1, device_id=device, device_id_type=MESH)
    pl.semaphore_wait(barrier, 3 + n_wt - 1)

    def block(at, size):
        return pl.ds(pl.multiple_of(at * size, 128), size)

    swap = remote(hid, hid_all.at[:, block(hd, half)], sem_h, sib)
    load_h.wait()
    swap.start()
    hid_all[:, block(hd, half)] = hid[...]
    small[:n_wt] = jnp.zeros((n_wt,) + small.shape[1:], F32)

    @pl.when(me == 0)
    def _():
        e_in[...] = jnp.zeros_like(e_in)
        prev_b[...] = jnp.zeros_like(prev_b)

    @pl.when(me == count - 1)
    def _():
        next_b[...] = jnp.zeros_like(next_b)

    swap.wait()
    floats = hid_all[...].astype(F32)
    scale = lax.rsqrt(jnp.mean(floats * floats, axis=-1, keepdims=True) + EPS)
    normed[...] = (floats * scale * norm_gain[...]).astype(BF)
    sends = []
    for k in range(1, n_wt):
        sends.append(remote(normed.at[:, block(lax.rem(w + k, n_wt), depth)], rows.at[k],
                            sem_r.at[k], peer(k)))
        sends[-1].start()
    rows[0] = normed[:, block(w, depth)]
    load_b.wait()
    load_x.wait()
    tiles, tile = prod.shape[1], prod.shape[3]
    backs = []

    def prod_copy(k, i):
        return remote(prod.at[k, i], prod.at[n_wt - 1 + k, i],
                      sem_p.at[k, i], peer(-k))

    for k in range(n_wt):
        if k:
            sends[k - 1].wait()

        n_bc = wbc.shape[1]
        bcs[k] = dot(rows[k], wbc[...]).astype(BF)
        small[k, :, :heads] = lax.dot_general(
            rows[k], wdt[...], (((1,), (1,)), ((), ())), preferred_element_type=F32)
        if k:
            backs.append(remote(small.at[k], small.at[n_wt - 1 + k], sem_s.at[k], peer(-k)))
            backs.append(remote(bcs.at[k], bcs.at[n_wt - 1 + k], sem_b.at[k], peer(-k)))
            backs[-2].start()
            backs[-1].start()

        @pl.loop(0, tiles)
        def _(i):
            prod[k, i] = dot(rows[k], wx[:, block(i, tile)]).astype(BF)
            if k:
                prod_copy(k, i).start()

    s_sum, bc_sum = small[0], bcs[0].astype(F32)
    for k in range(1, n_wt):
        backs[2 * k - 2].wait()
        backs[2 * k - 1].wait()
        s_sum = s_sum + small[n_wt - 1 + k]
        bc_sum = bc_sum + bcs[n_wt - 1 + k].astype(F32)
    n_state = n_bc // 2
    bc = silu(bc_sum)
    b, c = bc[:, :n_state].astype(BF), bc[:, n_state:].astype(BF)
    t_at = lax.broadcasted_iota(jnp.int32, (tokens, 128), 0)
    raw = s_sum + params[0:1, :]
    soft = jnp.maximum(raw, 0.0) + jnp.log1p(jnp.exp(-jnp.abs(raw)))
    dt = jnp.where(t_at < lengths[0], soft, 0.0)
    log = -dt * jnp.exp(params[1:2, :])
    lower = t_at >= lax.broadcasted_iota(jnp.int32, (tokens, tokens), 1)
    cum = jnp.dot(lower.astype(F32), log, precision=lax.Precision.HIGHEST, preferred_element_type=F32)
    cum_t[...] = cum.T
    dt_t[...] = dt.T
    b_f, c_f = b.astype(F32), c.astype(F32)
    b_t = b_f.T
    scores = dot(c, b_t.astype(BF))

    def head_cols(h):
        return block(h, 128)

    def one_head(h, i, j):
        at, cut = head_cols(h), slice(j * 128, (j + 1) * 128)
        total = prod[0, i, :, cut].astype(F32)
        for k in range(1, n_wt):
            total = total + prod[n_wt - 1 + k, i, :, cut].astype(F32)
        x_h = silu(total).astype(BF)
        row = cum_t[pl.ds(h, 1), :]
        dt_row = dt_t[pl.ds(h, 1), :]
        tail = jnp.exp(row[:, tokens - 1:] - row) * dt_row
        fresh[h] = dot((b_t * tail).astype(BF), x_h)
        wide = jnp.broadcast_to(row, (tokens, tokens))
        tall = wide.T
        decay = jnp.exp(jnp.where(lower, tall - wide, -jnp.inf))
        y = dot((scores * decay * dt_row).astype(BF), x_h)
        y_loc[:, at] = y + d_skip[h] * x_h.astype(F32)
        grow[h] = (c_f * jnp.exp(tall)).astype(BF)

    per_tile = tile // 128

    def state_copy(h):
        return remote(e_out.at[h], e_in.at[h], sem_e.at[h], shard(1))

    def y_copy(h, k):
        return remote(yh.at[0, h], yh.at[k, h], sem_y.at[h, k], peer(k))

    def chain_head(h):
        at = head_cols(h)
        row = cum_t[pl.ds(h, 1), :]
        @pl.when(me > 0)
        def _():
            state_copy(h).wait_recv()

        entering = e_in[h]

        @pl.when(me < count - 1)
        def _():
            e_out[h] = (jnp.exp(row[:, tokens - 1:]) * entering.astype(F32) + fresh[h]).astype(BF)
            state_copy(h).start()

        y = y_loc[:, at] + dot(grow[h], entering)
        scaling = lax.rsqrt(jnp.mean(y * y, axis=-1, keepdims=True) + EPS)
        y_h = (y * scaling * inner_gain[0:1, at]).astype(BF)
        yb[0, :, at] = y_h
        yh[0, h] = y_h
        for k in range(1, n_wt):
            y_copy(h, k).start()

    @pl.loop(0, tiles)
    def _(i):
        for k in range(1, n_wt):
            prod_copy(k, i).wait()
        for j in range(per_tile):
            one_head(i * per_tile + j, i, j)

        @pl.loop(0, per_tile)
        def _(j):
            chain_head(i * per_tile + j)

    @pl.when(me < count - 1)
    def _():
        @pl.loop(0, heads)
        def _(h):
            state_copy(h).wait_send()

    load_o.wait()
    o_tile = min(256, cols)
    o_copies = []
    for k in range(n_wt):
        if k:
            @pl.loop(0, heads)
            def _(h):
                y_copy(h, k).wait()
                yb[k, :, head_cols(h)] = yh[k, h]

        @pl.loop(0, cols // o_tile)
        def _(i):
            po[k, :, block(i, o_tile)] = dot(yb[k], wo[:, block(i, o_tile)]).astype(BF)

        if k:
            o_copies.append(remote(po.at[k], partial.at[:, block(w, cols)], sem_o.at[k], peer(-k)))
            o_copies[-1].start()
        else:
            partial[:, block(w, cols)] = po[0]
    for copy in o_copies:
        copy.wait()
    give = remote(partial.at[:, block(1 - hd, half)], hrec, sem_g, sib)
    give.start()
    base = hid[...].astype(F32) + partial[:, block(hd, half)].astype(F32)
    give.wait()
    mixed[...] = (base + hrec[...].astype(F32)).astype(BF)
    up = remote(mixed, prev_b, sem_n.at[0], shard(1))
    down = remote(mixed, next_b, sem_n.at[1], shard(-1))

    @pl.when(me < count - 1)
    def _():
        up.start()

    @pl.when(me > 0)
    def _():
        down.start()

    own = mixed[...].astype(F32) * (1.0 + mix[1])

    @pl.when(me > 0)
    def _():
        up.wait_recv()
        down.wait_send()

    @pl.when(me < count - 1)
    def _():
        down.wait_recv()
        up.wait_send()

    out[...] = (own + mix[0] * prev_b[...].astype(F32)
                + mix[2] * next_b[...].astype(F32)).astype(BF)


def body(hidden, norm_gain, w_x, w_bc, w_dt, dt_bias, a_log, d_skip, inner_gain, w_out,
         lengths, mix_index, mix_gain):
    tokens, half = hidden.shape
    width = norm_gain.shape[0]
    depth, chan = w_x.shape
    heads = w_dt.shape[1]
    size = chan // heads
    n_seq, n_wt = lax.axis_size("seq"), lax.axis_size("wt")
    cols = w_out.shape[1]
    slots = 2 * n_wt - 1
    vm, anyw = pl.BlockSpec(memory_space=pltpu.VMEM), pl.BlockSpec(memory_space=pl.ANY)
    V, sm = pltpu.VMEM, pl.BlockSpec(memory_space=pltpu.SMEM)
    tile = min(512, chan)
    return pl.pallas_call(
        functools.partial(kernel, n_seq, n_wt, heads),
        out_shape=jax.ShapeDtypeStruct((tokens, half), BF),
        in_specs=[anyw, vm, vm, sm, sm, sm, sm, vm, vm, anyw, anyw, vm, anyw],
        out_specs=vm,
        scratch_shapes=[
            V((tokens, half), BF), V(w_bc.shape, BF), V((8, 128), F32), V((tokens, chan), F32),
            V((heads, tokens, size), BF),
            V((tokens, width), BF), V((tokens, width), BF), V((n_wt, tokens, depth), BF),
            V((slots, chan // tile, tokens, tile), BF), V((slots, tokens, 128), F32),
            V((slots, tokens, w_bc.shape[1]), BF),
            V((depth, chan), BF), V((chan, cols), BF),
            V((128, tokens), F32), V((128, tokens), F32), V((heads, size, size), F32),
            V((heads, size, size), BF), V((heads, size, size), BF), V((n_wt, tokens, chan), BF),
            V((n_wt, heads, tokens, size), BF),
            V((n_wt, tokens, cols), BF), V((tokens, width), BF), V((tokens, half), BF),
            V((tokens, half), BF), V((tokens, half), BF), V((tokens, half), BF),
            DMA((4,)), DMA((2,)), DMA((n_wt, 2)), DMA((n_wt, chan // 128, 2)), DMA((n_wt, 2)), DMA((n_wt, 2)), DMA((heads, 2)),
            DMA((heads, n_wt, 2)), DMA((n_wt, 2)), DMA((2,)), DMA((2, 2)),
        ],
        compiler_params=pltpu.CompilerParams(
            collective_id=0, has_side_effects=True, vmem_limit_bytes=63 * 2**20
        ),
    )(hidden, dt_bias[None, :], a_log[None, :], d_skip, lengths, mix_index, mix_gain, norm_gain[None, :],
      inner_gain[None, :], w_x, w_bc, w_dt.T, w_out)


def solution(mesh):
    in_specs = (
        P(("grp", "seq", "wt"), "head"), P(), P("wt", "head"), P("wt", "head"), P("wt", "head"),
        P("head"), P("head"), P("head"), P("head"), P("head", "wt"),
        P(("grp", "seq", "wt")), P(("grp", "seq", "wt"), None), P(("grp", "seq", "wt"), None),
    )
    return jax.shard_map(
        body, mesh=mesh, in_specs=in_specs, out_specs=P(("grp", "seq", "wt"), "head"), check_vma=False
    )
```
